256 devices in a mesh: blk: 4 (over x), width: 16 (over z, core), rep: 4 (over y).
Axes of the slice: x: 4, y: 4, z: 8, core: 2. Of those that a mesh axis runs over, the one named last changes fastest.
Arguments:
- inputs: bfloat16 [2048, 7168], P(('blk', 'rep'), 'width'), may hold values from -6 to 6
- targets: bfloat16 [2048, 7168], P(('blk', 'rep'), 'width'), may hold values from -48 to 48
- enc_weight: bfloat16 [7168, 2048], P('width', 'blk'), may hold values from -0.0625 to 0.0625
- enc_bias: float32 [2048], P('blk'), may hold values from -3 to 3
- dec_weight: bfloat16 [2048, 7168], P('blk', 'width'), may hold values from -0.125 to 0.125
- dead_mask: int32 [2048], P('blk'), may hold values 0 or 1
- aux_picks: int32 [2048, 512], P(('blk', 'rep')), may hold values from 0 to 2047, all different within a row
Outputs:
- loss: float32 [], replicated
- grad_enc: float32 [7168, 2048], P(('width', 'rep'), 'blk')
- grad_bias: float32 [2048], P(('blk', 'rep'))
- grad_dec: float32 [2048, 7168], P('blk', ('width', 'rep'))
The draws below stay inside these ranges and needn't reach their ends.
Inputs may be any that keep to these rules, and one draw needn't show every extreme that they name: `aux_picks`: each row names 512 different latents; every latent is named by some row.
All inputs are finite; a program needn't handle non-finite values. No bound on the sum of `dead_mask` on one device may be relied on, other than what follows from the above.
Results may differ from the reference program's by a relative error of at most 0.025.
Values may be sent and summed in bfloat16 or wider, within the bound.
No kernel may reach another device: no remote copies, remote signals or barrier semaphores. Data moves between devices by JAX's collectives and lax.ppermute only.
A program may use at most 64 MiB of HBM per device.

```python
import jax
import jax.numpy as jnp
from jax import lax

D = 7168
TOK_BLK = 128
KAUX = 512
LATENTS = 2048
TOKENS = 2048
N_BLK = 4
N_REP = 4


def draw_targets(key, part):
    key = jax.random.fold_in(key, 7)
    key_base, key_rows, key_cols = jax.random.split(key, 3)
    row_pos = jnp.arange(TOKENS, dtype=jnp.float32)[:, None] / TOKENS
    col_pos = jnp.arange(D, dtype=jnp.float32)[None, :] / D
    rising = jnp.exp(0.5 * jnp.log(3.0) * (row_pos - 0.5)) * jnp.exp(0.5 * jnp.log(3.0) * (col_pos - 0.5))
    base = jax.random.normal(key_base, (TOKENS, D), jnp.float32)
    rows = jnp.exp(jax.random.uniform(key_rows, (TOKENS, 1), jnp.float32, -1.15, 1.15))
    cols = jnp.exp(jax.random.uniform(key_cols, (1, D), jnp.float32, -1.15, 1.15))
    values = jnp.clip(base * rows * cols * rising, -48.0, 48.0)
    return values.astype(jnp.bfloat16)


def set_ends(result, stream_key, smallest, high):
    shape = result.shape
    place = [jax.random.randint(jax.random.fold_in(stream_key, axis), (), 0, shape[axis]) for axis in range(len(shape))]
    result = result.at[tuple(place)].set(smallest)
    longest = shape.index(max(shape))
    place[longest] = (place[longest] + 1) % shape[longest]
    return result.at[tuple(place)].set(high)


def steps_of(rng, shape, cuts, least, largest):
    factor_of, own = 1.0, jax.random.fold_in(rng, 6)
    for axis_at, blocks in cuts:
        draws = jnp.exp(jax.random.uniform(jax.random.fold_in(own, axis_at), (blocks,), jnp.float32, least / len(cuts), largest / len(cuts)))
        factor_of = factor_of * jnp.repeat(draws, shape[axis_at] // blocks).reshape([-1 if axis == axis_at else 1 for axis in range(len(shape))])
    return factor_of


def different_ones(key, rows, amount, top, lift):
    sequence = jax.random.permutation(jax.random.fold_in(key, 1), amount)
    pull = sequence
    for power in range(3):
        pull = pull * pull // amount
    pull = pull * lift // amount
    chance = jax.random.randint(jax.random.fold_in(key, 2), (rows, amount), 0, 4096) + pull
    sure = jax.random.permutation(jax.random.fold_in(key, 3), rows)[jnp.arange(amount) % rows]
    chance = jnp.where(jnp.arange(rows)[:, None] == sure[None, :], 1 << 14, chance)
    score = chance * amount + jnp.arange(amount)
    return lax.top_k(score.astype(jnp.int32), top)[1].astype(jnp.int32)


def normal_values(key, dims, spread, bound, cuts=(), kind=jnp.bfloat16):
    factor_of = steps_of(key, dims, cuts, -0.22, 0.18) if cuts else 1.0
    result = jax.random.normal(key, dims, jnp.float32) * spread * factor_of
    return jnp.minimum(jnp.maximum(result, -bound), bound).astype(kind)


def setup_inputs(seed: int = 0) -> dict:
    streams_of = jax.random.split(jax.random.key(seed), 8)
    return {
        "inputs": normal_values(streams_of[0], (TOKENS, D), 1.0, 6.0, ((0, 16), (1, 16))),
        "targets": draw_targets(jax.random.fold_in(streams_of[7], 71), 0),
        "enc_weight": normal_values(streams_of[2], (D, LATENTS), D ** -0.5, 0.0625, ((0, 16), (1, 4))),
        "enc_bias": normal_values(streams_of[3], (LATENTS,), 0.5, 3.0, ((0, 4),), jnp.float32),
        "dec_weight": normal_values(streams_of[4], (LATENTS, D), LATENTS ** -0.5, 0.125, ((0, 4), (1, 16))),
        "dead_mask": set_ends((jax.random.randint(streams_of[5], (LATENTS,), 0, 2) < 1).astype(jnp.int32), jax.random.fold_in(streams_of[5], 1), 0, 1),
        "aux_picks": different_ones(streams_of[6], TOKENS, LATENTS, KAUX, 0),
    }


def reference(inputs, targets, enc_weight, enc_bias, dec_weight, dead_mask, aux_picks):
    preact = jnp.dot(inputs, enc_weight, preferred_element_type=jnp.float32) + enc_bias[None, :]
    latents = jnp.maximum(preact, 0.0).astype(jnp.bfloat16)
    token_ids = jnp.arange(TOKENS, dtype=jnp.int32)[:, None]
    picked = jnp.zeros((TOKENS, LATENTS), jnp.float32).at[token_ids, aux_picks].set(1.0)
    aux_gate = picked * jnp.where(dead_mask == 1, 1.0, 0.0).astype(jnp.float32)[None, :]
    aux_latents = latents * aux_gate.astype(jnp.bfloat16)
    recon = jnp.dot(latents, dec_weight, preferred_element_type=jnp.float32)
    recon_aux = jnp.dot(aux_latents, dec_weight, preferred_element_type=jnp.float32)
    error = targets.astype(jnp.float32) - recon
    error_aux = error - recon_aux
    loss = (jnp.sum(error * error) + jnp.sum(error_aux * error_aux)) / (TOKENS * D)
    norm_scale = 1.0 / jnp.sqrt(jnp.float32(TOKENS))
    grad_main = (-error * norm_scale).astype(jnp.bfloat16)
    grad_aux = (-error_aux * norm_scale).astype(jnp.bfloat16)
    pulled_main = jnp.dot(grad_main, dec_weight.T, preferred_element_type=jnp.float32)
    pulled_aux = jnp.dot(grad_aux, dec_weight.T, preferred_element_type=jnp.float32)
    grad_pre = jnp.where(preact > 0.0, pulled_main + aux_gate * pulled_aux, 0.0)
    grad_pre_b = grad_pre.astype(jnp.bfloat16)

    def split_rep(array):
        return array.reshape((N_BLK, N_REP, TOK_BLK) + array.shape[1:])
    inputs_r = split_rep(inputs)
    pre_r = split_rep(grad_pre)
    pre_b_r = split_rep(grad_pre_b)
    lat_r = split_rep(latents)
    aux_r = split_rep(aux_latents)
    main_r = split_rep(grad_main)
    gaux_r = split_rep(grad_aux)
    grad_enc = jnp.zeros((D, LATENTS), jnp.float32)
    grad_dec = jnp.zeros((LATENTS, D), jnp.float32)
    grad_bias = jnp.zeros((LATENTS,), jnp.float32)
    for replica in range(N_REP):
        x_rows = inputs_r[:, replica].reshape(-1, D)
        enc_term = jnp.dot(x_rows.T, pre_b_r[:, replica].reshape(-1, LATENTS), preferred_element_type=jnp.float32)
        dec_term = jnp.dot(lat_r[:, replica].reshape(-1, LATENTS).T, main_r[:, replica].reshape(-1, D), preferred_element_type=jnp.float32)
        dec_term = dec_term + jnp.dot(aux_r[:, replica].reshape(-1, LATENTS).T, gaux_r[:, replica].reshape(-1, D), preferred_element_type=jnp.float32)
        bias_term = lax.optimization_barrier(jnp.sum(pre_r[:, replica].reshape(-1, LATENTS), axis=0))
        grad_enc = grad_enc + enc_term.astype(jnp.bfloat16).astype(jnp.float32)
        grad_dec = grad_dec + dec_term.astype(jnp.bfloat16).astype(jnp.float32)
        grad_bias = grad_bias + bias_term.astype(jnp.bfloat16).astype(jnp.float32)
    return (loss, grad_enc, grad_bias, grad_dec)
```

```python
import math

import jax
import jax.numpy as jnp
from jax import lax
from jax.experimental import pallas as pl
from jax.experimental.pallas import tpu as pltpu
from jax.sharding import Mesh, PartitionSpec as P

F32 = jnp.float32
BF16 = jnp.bfloat16
GROUP = ("blk", "z", "core")


def from_ahead(block, axis, distance):
    size = lax.axis_size(axis)
    return lax.ppermute(block, axis, [((i + distance) % size, i) for i in range(size)])


def swap_core(block):
    return lax.ppermute(block, "core", [(0, 1), (1, 0)])


def shift_pieces(piece, sign):
    blk, z_size, cores = (lax.axis_size(name) for name in GROUP)
    half = z_size // 2
    route = []
    for b in range(blk):
        for z in range(z_size):
            for c in range(cores):
                to = (b + sign * (2 * c + z // half)) % blk
                route.append(((b * z_size + z) * cores + c, (to * z_size + z) * cores + c))
    return lax.ppermute(piece, GROUP, route)


def gather_z(piece):
    size = lax.axis_size("z")
    copies = jnp.broadcast_to(piece[None], (size,) + piece.shape)
    return lax.all_to_all(copies, "z", 0, 0, tiled=True)


def in_core_order(mine, other, core):
    first = jnp.where(core == 0, mine, other)
    second = jnp.where(core == 0, other, mine)
    return first, second


def pick_kernel(own_ref, picks_ref, out_ref, word_ref, bit_ref):
    own = own_ref[0]
    picks = picks_ref[...]
    place = (((own - (picks >> 9)) & 3) << 9) | (picks & 511)
    turned = jnp.transpose(place)
    word_ref[...] = turned >> 5
    bit_ref[...] = jnp.left_shift(jnp.int32(1), turned & 31)
    rows = picks_ref.shape[0]
    level = lax.broadcasted_iota(jnp.int32, (32, rows), 0)

    @pl.loop(0, out_ref.shape[1] // 128)
    def _(block):
        bits = []
        for sub in range(4):
            hit = word_ref[...] == block * 4 + sub
            total = jnp.sum(jnp.where(hit, bit_ref[...], 0), axis=0, keepdims=True)
            bits.append((jnp.broadcast_to(total, (32, rows)) >> level) & 1)
        square = jnp.concatenate(bits, 0).astype(F32)
        start = pl.multiple_of(block * 128, 128)
        out_ref[:, pl.ds(start, 128)] = jnp.transpose(square).astype(BF16)


def picked_latents(picks, own, lat_all):
    rows, count = picks.shape
    return pl.pallas_call(
        pick_kernel,
        out_shape=jax.ShapeDtypeStruct((rows, lat_all), BF16),
        in_specs=[
            pl.BlockSpec(memory_space=pltpu.SMEM),
            pl.BlockSpec(memory_space=pltpu.VMEM),
        ],
        out_specs=pl.BlockSpec(memory_space=pltpu.VMEM),
        scratch_shapes=[
            pltpu.VMEM((count, rows), jnp.int32),
            pltpu.VMEM((count, rows), jnp.int32),
        ],
        cost_estimate=pl.CostEstimate(flops=20_000_000, bytes_accessed=1_000_000, transcendentals=0),
    )(own.reshape(1).astype(jnp.int32), picks)


def two_halves(value):
    high = lax.reduce_precision(value, 8, 7)
    return high.astype(BF16), (value - high).astype(BF16)


def local(inputs, targets, enc_weight, enc_bias, dec_weight, dead_mask, aux_picks):
    blk, z_size, rep = lax.axis_size("blk"), lax.axis_size("z"), lax.axis_size("rep")
    core, blk_at, rep_at = lax.axis_index("core"), lax.axis_index("blk"), lax.axis_index("rep")
    rows, width = inputs.shape
    lat = dec_weight.shape[0]
    lat_all = blk * lat
    piece = rows * blk // (2 * z_size)
    total_tokens = rows * blk * rep
    norm_scale = 1.0 / math.sqrt(total_tokens)

    x_1, x_3 = from_ahead(inputs, "blk", 1), from_ahead(inputs, "blk", 3)
    x_2 = from_ahead(inputs, "blk", 2)
    dead = dead_mask.astype(BF16)
    dead_all = jnp.concatenate([dead] + [from_ahead(dead, "blk", -j) for j in (1, 2, 3)])
    picked = picked_latents(aux_picks, blk_at, lat_all)
    x_all = jnp.concatenate([inputs, x_1, x_2, x_3], 0)
    dec_own = lax.optimization_barrier((dec_weight, x_1, x_2, x_3))[0]
    dec_all = jnp.concatenate([dec_weight] + [from_ahead(dec_own, "blk", -j) for j in (1, 2, 3)], 0)

    halves = x_all.reshape(2, 2 * rows, width)
    sent = jnp.dot(
        lax.dynamic_index_in_dim(halves, 1 - core, 0, False), enc_weight, preferred_element_type=F32
    )
    got = swap_core(sent)
    kept = jnp.dot(
        lax.dynamic_index_in_dim(halves, core, 0, False), enc_weight, preferred_element_type=F32
    )
    parts = lax.all_to_all((kept + got).reshape(z_size, piece, lat), "z", 0, 0, tiled=True)
    preact = jnp.sum(parts, axis=0) + enc_bias[None, :]
    lat_piece = shift_pieces(jnp.maximum(preact, 0.0).astype(BF16), 1)

    lat_mine = gather_z(lat_piece).reshape(2, rows, lat)
    first, second = in_core_order(lat_mine, swap_core(lat_mine), core)
    latents = jnp.concatenate([first[0], first[1], second[0], second[1]], 1)
    gate = picked * dead_all[None, :]
    both = jnp.concatenate([latents, latents * gate], 0)

    decoded = jnp.dot(both, dec_all, preferred_element_type=F32)
    error = targets.astype(F32) - decoded[:rows]
    error_aux = error - decoded[rows:]
    loss_part = jnp.sum(error * error) + jnp.sum(error_aux * error_aux)
    loss_part = (loss_part + swap_core(loss_part.reshape(1, 1))[0, 0]).reshape(1, 1)
    grads = jnp.concatenate(
        [(-error * norm_scale).astype(BF16), (-error_aux * norm_scale).astype(BF16)], 0
    )

    def pulled_half(which):
        weight = lax.dynamic_slice_in_dim(dec_all, which * 2 * lat, 2 * lat, 0)
        opened = lax.dynamic_slice_in_dim(gate, which * 2 * lat, 2 * lat, 1).astype(F32)
        pulled = lax.dot_general(grads, weight, (((1,), (1,)), ((), ())), preferred_element_type=F32)
        return pulled[:rows] + pulled[rows:] * opened

    got_pulled = swap_core(pulled_half(1 - core).astype(BF16))
    pulled_sum = pulled_half(core) + got_pulled.astype(F32)
    pulled_sum = jnp.stack([pulled_sum[:, :lat], pulled_sum[:, lat:]], 0).astype(BF16)
    loss_lanes = jnp.concatenate([part.reshape(1, 1) for part in two_halves(loss_part)], 1)
    loss_lanes = jnp.pad(loss_lanes, ((0, 0), (0, 126)))
    packet = jnp.concatenate(
        [
            pulled_sum.reshape(z_size, piece, lat),
            jnp.broadcast_to(loss_lanes[None], (z_size, piece, 128)),
        ],
        2,
    )
    dec_term = lax.dot_general(
        grads, both, (((0,), (0,)), ((), ())), preferred_element_type=F32
    ).astype(BF16)
    share = width // rep
    dec_shares = dec_term.reshape(rep, share, lat_all)

    def rep_sum(shares):
        total = lax.dynamic_index_in_dim(shares, rep_at, 0, False).astype(F32)
        for step in (1, 3, 2):
            outgoing = lax.dynamic_index_in_dim(shares, (rep_at + step) % rep, 0, False)
            total = total + from_ahead(outgoing, "rep", -step).astype(F32)
        return total

    dec_sum = rep_sum(dec_shares).astype(BF16)

    arrived = lax.all_to_all(packet, "z", 0, 0, tiled=True).astype(F32)
    arrived = jnp.sum(arrived, axis=0)
    grad_piece = jnp.where(lat_piece > 0, arrived[:, :lat], 0.0).astype(BF16)
    loss_width = arrived[0, lat] + arrived[0, lat + 1]
    grad_piece = shift_pieces(grad_piece, -1)

    def with_rows(body, rows_of_more):
        more = [row.reshape(1, -1) for row in rows_of_more]
        more = [jnp.pad(row, ((0, 0), (0, lat - row.shape[1]))) for row in more]
        filler = jnp.zeros((16 - len(more), lat), BF16)
        return jnp.concatenate([body] + more + [filler], 0)

    def loss_row(value):
        return jnp.concatenate([part.reshape(1) for part in two_halves(value)])

    own_row = loss_row(loss_width)
    dec_final = dec_sum[:, :lat].astype(F32)
    loss_blk = loss_width
    for j in (1, 3, 2):
        outgoing = with_rows(dec_sum[:, j * lat : (j + 1) * lat], [own_row])
        incoming = from_ahead(outgoing, "blk", j).astype(F32)
        dec_final = dec_final + incoming[:share]
        loss_blk = loss_blk + incoming[share, 0] + incoming[share, 1]
    grad_dec = jnp.transpose(dec_final)

    grad_mine = gather_z(grad_piece).reshape(2 * rows, lat)
    first, second = in_core_order(grad_mine, swap_core(grad_mine), core)
    grad_pre = jnp.concatenate([first, second], 0)
    enc_term = lax.dot_general(
        x_all, grad_pre, (((0,), (0,)), ((), ())), preferred_element_type=F32
    ).astype(BF16)
    bias_term = jnp.sum(grad_pre.astype(F32), axis=0).astype(BF16)
    last_row = loss_row(loss_blk)
    shares = [
        with_rows(enc_term[i * share : (i + 1) * share], [bias_term, last_row]) for i in range(rep)
    ]
    final = rep_sum(jnp.stack(shares, 0))
    grad_enc = final[:share]
    grad_bias = lax.dynamic_slice_in_dim(final[share], rep_at * (lat // rep), lat // rep, 0)
    loss = (final[share + 1, 0] + final[share + 1, 1]) / (total_tokens * width * 2 * z_size)
    return (loss, grad_enc, grad_bias, grad_dec)


def solution(mesh):
    sizes = mesh.shape
    fine = Mesh(
        mesh.devices.reshape(sizes["blk"], sizes["width"] // 2, 2, sizes["rep"]),
        ("blk", "z", "core", "rep"),
    )
    wide = ("z", "core")
    in_specs = (
        P(("blk", "rep"), wide),
        P(("blk", "rep"), wide),
        P(wide, "blk"),
        P("blk"),
        P("blk", wide),
        P("blk"),
        P(("blk", "rep"), None),
    )
    out_specs = (P(), P(wide + ("rep",), "blk"), P(("blk", "rep")), P("blk", wide + ("rep",)))
    return jax.shard_map(local, mesh=fine, in_specs=in_specs, out_specs=out_specs, check_vma=False)
```

```python
import math

import jax
import jax.numpy as jnp
from jax import lax
from jax.experimental import pallas as pl
from jax.experimental.pallas import tpu as pltpu
from jax.sharding import Mesh, PartitionSpec as P

F32 = jnp.float32
BF16 = jnp.bfloat16
GROUP = ("blk", "z", "core")


def from_ahead(block, axis, distance):
    size = lax.axis_size(axis)
    return lax.ppermute(block, axis, [((i + distance) % size, i) for i in range(size)])


def blk_move(block, slot, sign):
    blk, cores = lax.axis_size("blk"), lax.axis_size("core")
    route = []
    for b in range(blk):
        for c in range(cores):
            to = (b + sign * (slot + 2 * c)) % blk
            route.append((b * cores + c, to * cores + c))
    return lax.ppermute(block, ("blk", "core"), route)


def swap_core(block):
    return lax.ppermute(block, "core", [(0, 1), (1, 0)])


def shift_pieces(piece, sign):
    blk, z_size, cores = (lax.axis_size(name) for name in GROUP)
    half = z_size // 2
    route = []
    for b in range(blk):
        for z in range(z_size):
            for c in range(cores):
                to = (b + sign * (2 * c + z // half)) % blk
                route.append(((b * z_size + z) * cores + c, (to * z_size + z) * cores + c))
    return lax.ppermute(piece, GROUP, route)


def z_copies(piece):
    return jnp.broadcast_to(piece[None], (lax.axis_size("z"),) + piece.shape)


def exchange_z(copies):
    return lax.all_to_all(copies, "z", 0, 0, tiled=True)


def after(values, event):
    return lax.optimization_barrier((values, event))[0]


def pick_kernel(own_ref, picks_ref, out_ref, word_ref, bit_ref):
    own = own_ref[0]
    picks = picks_ref[...]
    place = (((own - (picks >> 9)) & 3) << 9) | (picks & 511)
    turned = jnp.transpose(place)
    word_ref[...] = turned >> 5
    bit_ref[...] = jnp.left_shift(jnp.int32(1), turned & 31)
    rows = picks_ref.shape[0]
    level = lax.broadcasted_iota(jnp.int32, (32, rows), 0)

    @pl.loop(0, out_ref.shape[1] // 128)
    def _(block):
        bits = []
        for sub in range(4):
            hit = word_ref[...] == block * 4 + sub
            total = jnp.sum(jnp.where(hit, bit_ref[...], 0), axis=0, keepdims=True)
            bits.append((jnp.broadcast_to(total, (32, rows)) >> level) & 1)
        square = jnp.concatenate(bits, 0).astype(F32)
        start = pl.multiple_of(block * 128, 128)
        out_ref[:, pl.ds(start, 128)] = jnp.transpose(square).astype(BF16)


def picked_latents(picks, own, lat_all):
    rows, count = picks.shape
    return pl.pallas_call(
        pick_kernel,
        out_shape=jax.ShapeDtypeStruct((rows, lat_all), BF16),
        in_specs=[
            pl.BlockSpec(memory_space=pltpu.SMEM),
            pl.BlockSpec(memory_space=pltpu.VMEM),
        ],
        out_specs=pl.BlockSpec(memory_space=pltpu.VMEM),
        scratch_shapes=[
            pltpu.VMEM((count, rows), jnp.int32),
            pltpu.VMEM((count, rows), jnp.int32),
        ],
        cost_estimate=pl.CostEstimate(flops=20_000_000_000, bytes_accessed=1_000_000, transcendentals=0),
    )(own.reshape(1).astype(jnp.int32), picks)


def two_halves(value):
    high = lax.reduce_precision(value, 8, 7)
    return [high.astype(BF16), (value - high).astype(BF16)]


def with_rows(body, rows):
    width = body.shape[1]
    rows = [jnp.pad(row, ((0, 0), (0, width - row.shape[1]))) for row in rows]
    filler = jnp.zeros((16 - len(rows), width), BF16)
    return jnp.concatenate([body] + rows + [filler], 0)


def local(inputs, targets, enc_weight, enc_bias, dec_weight, dead_mask, aux_picks):
    blk, z_size, rep = lax.axis_size("blk"), lax.axis_size("z"), lax.axis_size("rep")
    core, blk_at, rep_at = lax.axis_index("core"), lax.axis_index("blk"), lax.axis_index("rep")
    rows, width = inputs.shape
    lat = dec_weight.shape[0]
    lat_all = blk * lat
    piece = rows * blk // (2 * z_size)
    total_tokens = rows * blk * rep
    norm_scale = 1.0 / math.sqrt(total_tokens)

    def in_slots(own, slot_1, across, slot_3):
        size = own.shape[0]
        whole = jnp.zeros((4 * size,) + own.shape[1:], own.dtype)
        for block, slot in ((own, 2 * core), (slot_1, 1), (slot_3, 3), (across, 2 - 2 * core)):
            whole = lax.dynamic_update_slice_in_dim(whole, block, slot * size, 0)
        return whole

    x_1, x_3 = blk_move(inputs, 1, -1), blk_move(inputs, 3, -1)
    x_2 = from_ahead(inputs, "blk", 2)
    x_all = in_slots(inputs, x_1, x_2, x_3)
    dead = jnp.broadcast_to(dead_mask.astype(BF16)[:, None], (lat, 16))
    dec_own = jnp.concatenate([dec_weight, dead], 1)
    dec_sent = after(dec_own, x_1)
    dec_1, dec_3 = blk_move(dec_sent, 1, 1), blk_move(dec_sent, 3, 1)
    half = lat // 2
    picked = picked_latents(aux_picks, blk_at + 2 * core, lat_all)

    got = swap_core(jnp.dot(x_all[2 * rows :], enc_weight, preferred_element_type=F32))
    kept = jnp.dot(x_all[: 2 * rows], enc_weight, preferred_element_type=F32)
    parts = lax.all_to_all((kept + got).reshape(z_size, piece, lat), "z", 0, 0, tiled=True)
    preact = jnp.sum(parts, axis=0) + enc_bias[None, :]
    lat_piece = jnp.maximum(preact, 0.0).astype(BF16)
    lat_piece, picked, dec_1, dec_3 = lax.optimization_barrier((lat_piece, picked, dec_1, dec_3))
    dec_2 = [blk_move(dec_1[:half], 1, 1), blk_move(dec_3[half:], 3, 1)]
    lat_piece = shift_pieces(lat_piece, 1)
    dec_all = in_slots(dec_own, dec_1, jnp.concatenate(dec_2, 0), dec_3)
    gate = picked * dec_all[:, width][None, :]

    lat_mine = exchange_z(z_copies(lat_piece)).reshape(2, rows, lat)
    lat_other = swap_core(lat_mine)
    latents = jnp.concatenate([lat_mine[0], lat_mine[1], lat_other[0], lat_other[1]], 1)
    both = jnp.concatenate([latents, latents * gate], 0)

    decoded = jnp.dot(both, dec_all, preferred_element_type=F32)
    error = targets.astype(F32) - decoded[:rows, :width]
    error_aux = error - decoded[rows:, :width]
    squares = error * error + error_aux * error_aux
    squares = jnp.pad(squares, ((0, 0), (0, -width % 128)))
    squares = sum(squares[:, i : i + 128] for i in range(0, squares.shape[1], 128))
    loss_part = jnp.sum(squares, axis=0, keepdims=True)
    grads = jnp.concatenate(
        [(-error * norm_scale).astype(BF16), (-error_aux * norm_scale).astype(BF16)], 0
    )
    grads = jnp.pad(grads, ((0, 0), (0, dec_all.shape[1] - width)))

    def pulled_half(start):
        pulled = lax.dot_general(
            grads,
            dec_all[start : start + 2 * lat],
            (((1,), (1,)), ((), ())),
            preferred_element_type=F32,
        )
        return pulled[:rows] + pulled[rows:] * gate[:, start : start + 2 * lat].astype(F32)

    got_pulled = swap_core(pulled_half(2 * lat).astype(BF16)).astype(F32)
    pulled_sum = pulled_half(0) + got_pulled
    pulled_sum = jnp.stack([pulled_sum[:, :lat], pulled_sum[:, lat:]], 0).astype(BF16)
    loss_rows = jnp.concatenate(two_halves(loss_part), 0)
    loss_rows = jnp.pad(loss_rows, ((0, piece - 2), (0, 0)))
    packet = jnp.concatenate(
        [
            pulled_sum.reshape(z_size, piece, lat),
            jnp.broadcast_to(loss_rows[None], (z_size,) + loss_rows.shape),
        ],
        2,
    )
    arrived = lax.all_to_all(packet, "z", 0, 0, tiled=True).astype(F32)

    dec_term = lax.dot_general(
        after(grads, packet), both, (((0,), (0,)), ((), ())), preferred_element_type=F32
    ).astype(BF16)
    share = width // rep

    def rep_exchange(shares):
        own = lax.dynamic_index_in_dim(shares, rep_at, 0, False)
        parts = [own]
        for step in (1, 3, 2):
            outgoing = lax.dynamic_index_in_dim(shares, (rep_at + step) % rep, 0, False)
            parts.append(from_ahead(outgoing, "rep", -step))
        return parts

    dec_parts = rep_exchange(dec_term[:width].reshape(rep, share, lat_all))

    arrived = jnp.sum(arrived, axis=0)
    grad_piece = jnp.where(lat_piece > 0, arrived[:, :lat], 0.0).astype(BF16)
    loss_width = arrived[0:1, lat:] + arrived[1:2, lat:]
    grad_piece = shift_pieces(grad_piece, -1)
    loss_width = loss_width + swap_core(loss_width)
    grad_copies = z_copies(grad_piece)
    dec_sum = sum(part.astype(F32) for part in after(dec_parts, grad_copies)).astype(BF16)

    loss_out = two_halves(loss_width)
    dec_own_slot = lax.dynamic_slice_in_dim(dec_sum, core * 2 * lat, lat, 1)
    dec_across = lax.dynamic_slice_in_dim(dec_sum, (1 - core) * 2 * lat, lat, 1)
    incoming = [
        blk_move(with_rows(dec_sum[:, lat : 2 * lat], loss_out), 1, -1),
        blk_move(with_rows(dec_sum[:, 3 * lat :], loss_out), 3, -1),
        from_ahead(with_rows(dec_across, loss_out), "blk", 2),
    ]
    grad_mine = exchange_z(grad_copies).reshape(2 * rows, lat)
    incoming = after(incoming, grad_mine)
    dec_final = dec_own_slot.astype(F32) + sum(part[:share].astype(F32) for part in incoming)
    loss_blk = loss_width
    for part in incoming:
        both_rows = part[share : share + 2, :128].astype(F32)
        loss_blk = loss_blk + both_rows[0:1] + both_rows[1:2]
    grad_dec = jnp.transpose(dec_final)

    grad_pre = jnp.concatenate([grad_mine, swap_core(grad_mine)], 0)
    enc_term = lax.dot_general(
        x_all, grad_pre, (((0,), (0,)), ((), ())), preferred_element_type=F32
    ).astype(BF16)
    bias_term = jnp.sum(grad_pre.astype(F32), axis=0, keepdims=True).astype(BF16)
    loss_out = two_halves(loss_blk)
    quarter = lat // rep
    shares = [
        with_rows(
            enc_term[i * share : (i + 1) * share],
            [bias_term[:, i * quarter : (i + 1) * quarter]] + loss_out,
        )
        for i in range(rep)
    ]
    parts = rep_exchange(jnp.stack(shares, 0))
    grad_enc = sum(part[:share].astype(F32) for part in parts)
    last = sum(part[share : share + 3, :quarter].astype(F32) for part in parts)
    loss = jnp.sum(last[1:3]) / (total_tokens * width * 2 * z_size)
    return (loss, grad_enc, last[0], grad_dec)


def solution(mesh):
    sizes = mesh.shape
    fine = Mesh(
        mesh.devices.reshape(sizes["blk"], sizes["width"] // 2, 2, sizes["rep"]),
        ("blk", "z", "core", "rep"),
    )
    wide = ("z", "core")
    in_specs = (
        P(("blk", "rep"), wide),
        P(("blk", "rep"), wide),
        P(wide, "blk"),
        P("blk"),
        P("blk", wide),
        P("blk"),
        P(("blk", "rep"), None),
    )
    out_specs = (P(), P(wide + ("rep",), "blk"), P(("blk", "rep")), P("blk", wide + ("rep",)))
    return jax.shard_map(local, mesh=fine, in_specs=in_specs, out_specs=out_specs, check_vma=False)
```

```python
import math

import jax
import jax.numpy as jnp
from jax import lax
from jax.experimental import pallas as pl
from jax.experimental.pallas import tpu as pltpu
from jax.sharding import Mesh, PartitionSpec as P

F32 = jnp.float32
BF16 = jnp.bfloat16
GROUP = ("blk", "z", "core")


def from_ahead(block, axis, distance):
    size = lax.axis_size(axis)
    return lax.ppermute(block, axis, [((i + distance) % size, i) for i in range(size)])


def blk_move(block, slot, sign):
    blk, cores = lax.axis_size("blk"), lax.axis_size("core")
    route = []
    for b in range(blk):
        for c in range(cores):
            to = (b + sign * (slot + 2 * c)) % blk
            route.append((b * cores + c, to * cores + c))
    return lax.ppermute(block, ("blk", "core"), route)


def swap_core(block):
    return lax.ppermute(block, "core", [(0, 1), (1, 0)])


def shift_pieces(piece, sign):
    blk, z_size, cores = (lax.axis_size(name) for name in GROUP)
    half = z_size // 2
    route = []
    for b in range(blk):
        for z in range(z_size):
            for c in range(cores):
                to = (b + sign * (2 * c + z // half)) % blk
                route.append(((b * z_size + z) * cores + c, (to * z_size + z) * cores + c))
    return lax.ppermute(piece, GROUP, route)


def z_copies(piece):
    return jnp.broadcast_to(piece[None], (lax.axis_size("z"),) + piece.shape)


def exchange_z(copies):
    return lax.all_to_all(copies, "z", 0, 0, tiled=True)


def after(values, event):
    return lax.optimization_barrier((values, event))[0]


def pick_kernel(own_ref, picks_ref, out_ref, word_ref, bit_ref):
    own = own_ref[0]
    picks = picks_ref[...]
    place = (((own - (picks >> 9)) & 3) << 9) | (picks & 511)
    turned = jnp.transpose(place)
    word_ref[...] = turned >> 5
    bit_ref[...] = jnp.left_shift(jnp.int32(1), turned & 31)
    rows = picks_ref.shape[0]
    level = lax.broadcasted_iota(jnp.int32, (32, rows), 0)

    @pl.loop(0, out_ref.shape[1] // 128)
    def _(block):
        bits = []
        for sub in range(4):
            hit = word_ref[...] == block * 4 + sub
            total = jnp.sum(jnp.where(hit, bit_ref[...], 0), axis=0, keepdims=True)
            bits.append((jnp.broadcast_to(total, (32, rows)) >> level) & 1)
        square = jnp.concatenate(bits, 0).astype(F32)
        start = pl.multiple_of(block * 128, 128)
        out_ref[:, pl.ds(start, 128)] = jnp.transpose(square).astype(BF16)


def picked_latents(picks, own, lat_all):
    rows, count = picks.shape
    return pl.pallas_call(
        pick_kernel,
        out_shape=jax.ShapeDtypeStruct((rows, lat_all), BF16),
        in_specs=[
            pl.BlockSpec(memory_space=pltpu.SMEM),
            pl.BlockSpec(memory_space=pltpu.VMEM),
        ],
        out_specs=pl.BlockSpec(memory_space=pltpu.VMEM),
        scratch_shapes=[
            pltpu.VMEM((count, rows), jnp.int32),
            pltpu.VMEM((count, rows), jnp.int32),
        ],
        cost_estimate=pl.CostEstimate(flops=20_000_000, bytes_accessed=1_000_000, transcendentals=0),
    )(own.reshape(1).astype(jnp.int32), picks)


def two_halves(value):
    high = lax.reduce_precision(value, 8, 7)
    return [high.astype(BF16), (value - high).astype(BF16)]


def with_rows(body, rows):
    width = body.shape[1]
    rows = [jnp.pad(row, ((0, 0), (0, width - row.shape[1]))) for row in rows]
    filler = jnp.zeros((16 - len(rows), width), BF16)
    return jnp.concatenate([body] + rows + [filler], 0)


def local(inputs, targets, enc_weight, enc_bias, dec_weight, dead_mask, aux_picks):
    blk, z_size, rep = lax.axis_size("blk"), lax.axis_size("z"), lax.axis_size("rep")
    core, blk_at, rep_at = lax.axis_index("core"), lax.axis_index("blk"), lax.axis_index("rep")
    rows, width = inputs.shape
    lat = dec_weight.shape[0]
    lat_all = blk * lat
    piece = rows * blk // (2 * z_size)
    total_tokens = rows * blk * rep
    norm_scale = 1.0 / math.sqrt(total_tokens)

    def in_slots(own, slot_1, across, slot_3):
        size = own.shape[0]
        whole = jnp.zeros((4 * size,) + own.shape[1:], own.dtype)
        for block, slot in ((own, 2 * core), (slot_1, 1), (slot_3, 3), (across, 2 - 2 * core)):
            whole = lax.dynamic_update_slice_in_dim(whole, block, slot * size, 0)
        return whole

    x_1, x_3 = blk_move(inputs, 1, -1), blk_move(inputs, 3, -1)
    x_2 = from_ahead(inputs, "blk", 2)
    dead = jnp.broadcast_to(dead_mask.astype(BF16)[:, None], (lat, 16))
    dec_own = jnp.concatenate([dec_weight, dead], 1)
    dec_sent, x_2 = lax.optimization_barrier((dec_own, x_2))
    x_all = in_slots(inputs, x_1, x_2, x_3)
    dec_1, dec_3 = blk_move(dec_sent, 1, 1), blk_move(dec_sent, 3, 1)
    half = dec_own.shape[1] // 32 * 16
    picked = picked_latents(aux_picks, blk_at + 2 * core, lat_all)

    got = swap_core(jnp.dot(x_all[2 * rows :], enc_weight, preferred_element_type=F32))
    kept = jnp.dot(x_all[: 2 * rows], enc_weight, preferred_element_type=F32)
    parts = lax.all_to_all((kept + got).reshape(z_size, piece, lat), "z", 0, 0, tiled=True)
    preact = jnp.sum(parts, axis=0) + enc_bias[None, :]
    lat_piece = jnp.maximum(preact, 0.0).astype(BF16)
    lat_piece, picked = lax.optimization_barrier((lat_piece, picked))
    dec_1, dec_3 = after((dec_1, dec_3), lat_piece)
    dec_2 = [blk_move(dec_1[:, :half], 1, 1), blk_move(dec_3[:, half:], 3, 1)]
    lat_piece = shift_pieces(lat_piece, 1)
    dec_all = in_slots(dec_own, dec_1, jnp.concatenate(dec_2, 1), dec_3)
    gate = picked * dec_all[:, width][None, :]

    lat_mine = exchange_z(z_copies(lat_piece)).reshape(2, rows, lat)
    lat_other = swap_core(lat_mine)
    latents = jnp.concatenate([lat_mine[0], lat_mine[1], lat_other[0], lat_other[1]], 1)
    both = jnp.concatenate([latents, latents * gate], 0)

    decoded = jnp.dot(both, dec_all, preferred_element_type=F32)
    error = targets.astype(F32) - decoded[:rows, :width]
    error_aux = error - decoded[rows:, :width]
    squares = error * error + error_aux * error_aux
    squares = jnp.pad(squares, ((0, 0), (0, -width % 128)))
    squares = sum(squares[:, i : i + 128] for i in range(0, squares.shape[1], 128))
    loss_part = jnp.sum(squares, axis=0, keepdims=True)
    grads = jnp.concatenate(
        [(-error * norm_scale).astype(BF16), (-error_aux * norm_scale).astype(BF16)], 0
    )
    grads = jnp.pad(grads, ((0, 0), (0, dec_all.shape[1] - width)))

    def pulled_half(start):
        pulled = lax.dot_general(
            grads,
            dec_all[start : start + 2 * lat],
            (((1,), (1,)), ((), ())),
            preferred_element_type=F32,
        )
        return pulled[:rows] + pulled[rows:] * gate[:, start : start + 2 * lat].astype(F32)

    got_pulled = swap_core(pulled_half(2 * lat).astype(BF16)).astype(F32)
    pulled_sum = pulled_half(0) + got_pulled
    pulled_sum = jnp.stack([pulled_sum[:, :lat], pulled_sum[:, lat:]], 0).astype(BF16)
    loss_rows = jnp.concatenate(two_halves(loss_part), 0)
    loss_rows = jnp.pad(loss_rows, ((0, piece - 2), (0, 0)))
    packet = jnp.concatenate(
        [
            pulled_sum.reshape(z_size, piece, lat),
            jnp.broadcast_to(loss_rows[None], (z_size,) + loss_rows.shape),
        ],
        2,
    )
    arrived = lax.all_to_all(packet, "z", 0, 0, tiled=True).astype(F32)

    dec_term = lax.dot_general(
        after(grads, packet), both, (((0,), (0,)), ((), ())), preferred_element_type=F32
    ).astype(BF16)
    share = width // rep

    def rep_exchange(shares):
        own = lax.dynamic_index_in_dim(shares, rep_at, 0, False)
        parts = [own]
        for step in (1, 3, 2):
            outgoing = lax.dynamic_index_in_dim(shares, (rep_at + step) % rep, 0, False)
            parts.append(from_ahead(outgoing, "rep", -step))
        return parts

    dec_parts = rep_exchange(dec_term[:width].reshape(rep, share, lat_all))

    arrived = jnp.sum(arrived, axis=0)
    grad_piece = jnp.where(lat_piece > 0, arrived[:, :lat], 0.0).astype(BF16)
    loss_width = arrived[0:1, lat:] + arrived[1:2, lat:]
    grad_piece = shift_pieces(grad_piece, -1)
    loss_width = loss_width + swap_core(loss_width)
    grad_copies = z_copies(grad_piece)
    dec_sum = sum(part.astype(F32) for part in after(dec_parts, grad_copies)).astype(BF16)

    loss_out = two_halves(loss_width)
    dec_own_slot = lax.dynamic_slice_in_dim(dec_sum, core * 2 * lat, lat, 1)
    dec_across = lax.dynamic_slice_in_dim(dec_sum, (1 - core) * 2 * lat, lat, 1)
    incoming = [
        blk_move(with_rows(dec_sum[:, lat : 2 * lat], loss_out), 1, -1),
        blk_move(with_rows(dec_sum[:, 3 * lat :], loss_out), 3, -1),
        from_ahead(with_rows(dec_across, loss_out), "blk", 2),
    ]

    grad_mine = exchange_z(grad_copies).reshape(2 * rows, lat)
    incoming = after(incoming, grad_mine)
    dec_final = dec_own_slot.astype(F32) + sum(part[:share].astype(F32) for part in incoming)
    loss_blk = loss_width
    for part in incoming:
        both_rows = part[share : share + 2, :128].astype(F32)
        loss_blk = loss_blk + both_rows[0:1] + both_rows[1:2]
    grad_dec = jnp.transpose(dec_final)
    grad_pre = jnp.concatenate([grad_mine, swap_core(grad_mine)], 0)
    enc_term = lax.dot_general(
        x_all, grad_pre, (((0,), (0,)), ((), ())), preferred_element_type=F32
    ).astype(BF16)
    bias_term = jnp.sum(grad_pre.astype(F32), axis=0, keepdims=True).astype(BF16)

    quarter = lat // rep
    more = [bias_term.reshape(rep, 1, quarter)]
    more += [jnp.broadcast_to(row[None], (rep,) + row.shape) for row in two_halves(loss_blk)]
    more = [jnp.pad(row, ((0, 0), (0, 0), (0, lat - row.shape[2]))) for row in more]
    more.append(jnp.zeros((rep, 13, lat), BF16))
    parts = rep_exchange(jnp.concatenate([enc_term.reshape(rep, share, lat)] + more, 1))
    grad_enc = sum(part[:share].astype(F32) for part in parts)
    last = sum(part[share : share + 3, :quarter].astype(F32) for part in parts)
    loss = jnp.sum(last[1:3]) / (total_tokens * width * 2 * z_size)
    return (loss, grad_enc, last[0], grad_dec)


def solution(mesh):
    sizes = mesh.shape
    fine = Mesh(
        mesh.devices.reshape(sizes["blk"], sizes["width"] // 2, 2, sizes["rep"]),
        ("blk", "z", "core", "rep"),
    )
    wide = ("z", "core")
    in_specs = (
        P(("blk", "rep"), wide),
        P(("blk", "rep"), wide),
        P(wide, "blk"),
        P("blk"),
        P("blk", wide),
        P("blk"),
        P(("blk", "rep"), None),
    )
    out_specs = (P(), P(wide + ("rep",), "blk"), P(("blk", "rep")), P("blk", wide + ("rep",)))
    return jax.shard_map(local, mesh=fine, in_specs=in_specs, out_specs=out_specs, check_vma=False)
```

```python
import math

import jax
import jax.numpy as jnp
from jax import lax
from jax.experimental import pallas as pl
from jax.experimental.pallas import tpu as pltpu
from jax.sharding import Mesh, PartitionSpec as P

F32 = jnp.float32
BF16 = jnp.bfloat16
GROUP = ("blk", "z", "core")


def from_ahead(block, axis, distance):
    size = lax.axis_size(axis)
    return lax.ppermute(block, axis, [((i + distance) % size, i) for i in range(size)])


def blk_move(block, slot, sign):
    blk, cores = lax.axis_size("blk"), lax.axis_size("core")
    route = []
    for b in range(blk):
        for c in range(cores):
            to = (b + sign * (slot + 2 * c)) % blk
            route.append((b * cores + c, to * cores + c))
    return lax.ppermute(block, ("blk", "core"), route)


def swap_core(block):
    return lax.ppermute(block, "core", [(0, 1), (1, 0)])


def shift_pieces(piece, sign):
    blk, z_size, cores = (lax.axis_size(name) for name in GROUP)
    half = z_size // 2
    route = []
    for b in range(blk):
        for z in range(z_size):
            for c in range(cores):
                to = (b + sign * (2 * c + z // half)) % blk
                route.append(((b * z_size + z) * cores + c, (to * z_size + z) * cores + c))
    return lax.ppermute(piece, GROUP, route)


def z_copies(piece):
    return jnp.broadcast_to(piece[None], (lax.axis_size("z"),) + piece.shape)


def exchange_z(copies):
    return lax.all_to_all(copies, "z", 0, 0, tiled=True)


def after(values, event):
    return lax.optimization_barrier((values, event))[0]


def pick_kernel(own_ref, picks_ref, out_ref, word_ref, bit_ref):
    own = own_ref[0]
    picks = picks_ref[...]
    place = (((own - (picks >> 9)) & 3) << 9) | (picks & 511)
    turned = jnp.transpose(place)
    word_ref[...] = turned >> 5
    bit_ref[...] = jnp.left_shift(jnp.int32(1), turned & 31)
    rows = picks_ref.shape[0]
    level = lax.broadcasted_iota(jnp.int32, (32, rows), 0)

    @pl.loop(0, out_ref.shape[1] // 128)
    def _(block):
        bits = []
        for sub in range(4):
            hit = word_ref[...] == block * 4 + sub
            total = jnp.sum(jnp.where(hit, bit_ref[...], 0), axis=0, keepdims=True)
            bits.append((jnp.broadcast_to(total, (32, rows)) >> level) & 1)
        square = jnp.concatenate(bits, 0).astype(F32)
        start = pl.multiple_of(block * 128, 128)
        out_ref[:, pl.ds(start, 128)] = jnp.transpose(square).astype(BF16)


def picked_latents(picks, own, lat_all):
    rows, count = picks.shape
    return pl.pallas_call(
        pick_kernel,
        out_shape=jax.ShapeDtypeStruct((rows, lat_all), BF16),
        in_specs=[
            pl.BlockSpec(memory_space=pltpu.SMEM),
            pl.BlockSpec(memory_space=pltpu.VMEM),
        ],
        out_specs=pl.BlockSpec(memory_space=pltpu.VMEM),
        scratch_shapes=[
            pltpu.VMEM((count, rows), jnp.int32),
            pltpu.VMEM((count, rows), jnp.int32),
        ],
        cost_estimate=pl.CostEstimate(flops=20_000_000, bytes_accessed=1_000_000, transcendentals=0),
    )(own.reshape(1).astype(jnp.int32), picks)


def two_halves(value):
    high = lax.reduce_precision(value, 8, 7)
    return [high.astype(BF16), (value - high).astype(BF16)]


def with_rows(body, rows):
    width = body.shape[1]
    rows = [jnp.pad(row, ((0, 0), (0, width - row.shape[1]))) for row in rows]
    filler = jnp.zeros((8 - len(rows), width), BF16)
    return jnp.concatenate([body] + rows + [filler], 0)


def local(inputs, targets, enc_weight, enc_bias, dec_weight, dead_mask, aux_picks):
    blk, z_size, rep = lax.axis_size("blk"), lax.axis_size("z"), lax.axis_size("rep")
    core, blk_at, rep_at = lax.axis_index("core"), lax.axis_index("blk"), lax.axis_index("rep")
    rows, width = inputs.shape
    lat = dec_weight.shape[0]
    lat_all = blk * lat
    piece = rows * blk // (2 * z_size)
    total_tokens = rows * blk * rep
    norm_scale = 1.0 / math.sqrt(total_tokens)

    def in_slots(own, slot_1, across, slot_3):
        size = own.shape[0]
        whole = jnp.zeros((4 * size,) + own.shape[1:], own.dtype)
        for block, slot in ((own, 2 * core), (slot_1, 1), (slot_3, 3), (across, 2 - 2 * core)):
            whole = lax.dynamic_update_slice_in_dim(whole, block, slot * size, 0)
        return whole

    x_1, x_3 = blk_move(inputs, 1, -1), blk_move(inputs, 3, -1)
    x_2 = from_ahead(inputs, "blk", 2)
    enc_far = swap_core(enc_weight)
    dead = jnp.broadcast_to(dead_mask.astype(BF16)[:, None], (lat, 16))
    dec_own = jnp.concatenate([dec_weight, dead], 1)
    dec_sent, x_2 = lax.optimization_barrier((dec_own, x_2))
    x_all = in_slots(inputs, x_1, x_2, x_3)
    dec_1, dec_3 = blk_move(dec_sent, 1, 1), blk_move(dec_sent, 3, 1)
    half = dec_own.shape[1] // 32 * 16
    picked = picked_latents(aux_picks, blk_at + 2 * core, lat_all)

    x_far = swap_core(x_all[2 * rows :])
    summed = jnp.dot(x_all[: 2 * rows], enc_weight, preferred_element_type=F32)
    summed = summed + jnp.dot(x_far, enc_far, preferred_element_type=F32)
    parts = exchange_z(summed.reshape(z_size, piece, lat))
    preact = jnp.sum(parts, axis=0) + enc_bias[None, :]
    lat_piece = jnp.maximum(preact, 0.0).astype(BF16)
    lat_piece, picked = lax.optimization_barrier((lat_piece, picked))
    dec_1, dec_3 = after((dec_1, dec_3), lat_piece)
    lat_piece = shift_pieces(lat_piece, 1)
    lat_piece, passed_1, passed_3 = lax.optimization_barrier(
        (lat_piece, dec_1[:, :half], dec_3[:, half:])
    )
    dec_2 = [blk_move(passed_1, 1, 1), blk_move(passed_3, 3, 1)]
    dec_all = in_slots(dec_own, dec_1, jnp.concatenate(dec_2, 1), dec_3)
    gate = picked * dec_all[:, width][None, :]

    lat_mine = exchange_z(z_copies(lat_piece)).reshape(2, rows, lat)
    lat_other = swap_core(lat_mine)
    latents = jnp.concatenate([lat_mine[0], lat_mine[1], lat_other[0], lat_other[1]], 1)
    both = jnp.concatenate([latents, latents * gate], 0)

    decoded = jnp.dot(both, dec_all, preferred_element_type=F32)
    error = targets.astype(F32) - decoded[:rows, :width]
    error_aux = error - decoded[rows:, :width]
    squares = error * error + error_aux * error_aux
    squares = jnp.pad(squares, ((0, 0), (0, -width % 128)))
    squares = sum(squares[:, i : i + 128] for i in range(0, squares.shape[1], 128))
    loss_part = jnp.sum(squares, axis=0, keepdims=True)
    grads = jnp.concatenate(
        [(-error * norm_scale).astype(BF16), (-error_aux * norm_scale).astype(BF16)], 0
    )
    grads = jnp.pad(grads, ((0, 0), (0, dec_all.shape[1] - width)))

    def pulled_half(start):
        pulled = lax.dot_general(
            grads,
            dec_all[start : start + 2 * lat],
            (((1,), (1,)), ((), ())),
            preferred_element_type=F32,
        )
        return pulled[:rows] + pulled[rows:] * gate[:, start : start + 2 * lat].astype(F32)

    got_pulled = swap_core(pulled_half(2 * lat).astype(BF16)).astype(F32)
    pulled_sum = pulled_half(0) + got_pulled
    pulled_sum = jnp.stack([pulled_sum[:, :lat], pulled_sum[:, lat:]], 0).astype(BF16)
    loss_rows = jnp.concatenate(two_halves(loss_part), 0)
    loss_rows = jnp.pad(loss_rows, ((0, piece - 2), (0, 0)))
    packet = jnp.concatenate(
        [
            pulled_sum.reshape(z_size, piece, lat),
            jnp.broadcast_to(loss_rows[None], (z_size,) + loss_rows.shape),
        ],
        2,
    )
    arrived = lax.all_to_all(packet, "z", 0, 0, tiled=True).astype(F32)

    dec_term = lax.dot_general(
        after(grads, packet), both, (((0,), (0,)), ((), ())), preferred_element_type=F32
    ).astype(BF16)
    share = width // rep

    def rep_exchange(shares):
        own = lax.dynamic_index_in_dim(shares, rep_at, 0, False)
        parts = [own]
        for step in (1, 3, 2):
            outgoing = lax.dynamic_index_in_dim(shares, (rep_at + step) % rep, 0, False)
            parts.append(from_ahead(outgoing, "rep", -step))
        return parts

    dec_parts = rep_exchange(dec_term[:width].reshape(rep, share, lat_all))

    arrived = jnp.sum(arrived, axis=0)
    grad_piece = jnp.where(lat_piece > 0, arrived[:, :lat], 0.0).astype(BF16)
    loss_width = arrived[0:1, lat:] + arrived[1:2, lat:]
    grad_piece = shift_pieces(grad_piece, -1)
    grad_copies = z_copies(grad_piece)
    loss_width = after(loss_width, grad_copies)
    loss_width = loss_width + swap_core(loss_width)
    dec_sum = sum(part.astype(F32) for part in after(dec_parts, grad_copies)).astype(BF16)

    loss_out = two_halves(loss_width)
    dec_own_slot = lax.dynamic_slice_in_dim(dec_sum, core * 2 * lat, lat, 1)
    dec_across = lax.dynamic_slice_in_dim(dec_sum, (1 - core) * 2 * lat, lat, 1)
    incoming = [
        blk_move(with_rows(dec_sum[:, lat : 2 * lat], loss_out), 1, -1),
        blk_move(with_rows(dec_sum[:, 3 * lat :], loss_out), 3, -1),
        from_ahead(with_rows(dec_across, loss_out), "blk", 2),
    ]

    grad_mine = exchange_z(grad_copies).reshape(2 * rows, lat)
    incoming = after(incoming, grad_mine)
    dec_final = dec_own_slot.astype(F32) + sum(part[:share].astype(F32) for part in incoming)
    loss_blk = loss_width
    for part in incoming:
        both_rows = part[share : share + 2, :128].astype(F32)
        loss_blk = loss_blk + both_rows[0:1] + both_rows[1:2]
    grad_dec = jnp.transpose(dec_final)
    grad_pre = jnp.concatenate([grad_mine, swap_core(grad_mine)], 0)
    enc_term = lax.dot_general(
        x_all, grad_pre, (((0,), (0,)), ((), ())), preferred_element_type=F32
    ).astype(BF16)
    bias_term = jnp.sum(grad_pre.astype(F32), axis=0, keepdims=True).astype(BF16)

    quarter = lat // rep
    more = [bias_term.reshape(rep, 1, quarter)]
    more += [jnp.broadcast_to(row[None], (rep,) + row.shape) for row in two_halves(loss_blk)]
    more = [jnp.pad(row, ((0, 0), (0, 0), (0, lat - row.shape[2]))) for row in more]
    more.append(jnp.zeros((rep, 5, lat), BF16))
    parts = rep_exchange(jnp.concatenate([enc_term.reshape(rep, share, lat)] + more, 1))
    grad_enc = sum(part[:share].astype(F32) for part in parts)
    last = sum(part[share : share + 3, :quarter].astype(F32) for part in parts)
    loss = jnp.sum(last[1:3]) / (total_tokens * width * 2 * z_size)
    return (loss, grad_enc, last[0], grad_dec)


def solution(mesh):
    sizes = mesh.shape
    fine = Mesh(
        mesh.devices.reshape(sizes["blk"], sizes["width"] // 2, 2, sizes["rep"]),
        ("blk", "z", "core", "rep"),
    )
    wide = ("z", "core")
    in_specs = (
        P(("blk", "rep"), wide),
        P(("blk", "rep"), wide),
        P(wide, "blk"),
        P("blk"),
        P("blk", wide),
        P("blk"),
        P(("blk", "rep"), None),
    )
    out_specs = (P(), P(wide + ("rep",), "blk"), P(("blk", "rep")), P("blk", wide + ("rep",)))
    return jax.shard_map(local, mesh=fine, in_specs=in_specs, out_specs=out_specs, check_vma=False)
```

```python
import math

import jax
import jax.numpy as jnp
from jax import lax
from jax.experimental import pallas as pl
from jax.experimental.pallas import tpu as pltpu
from jax.sharding import Mesh, PartitionSpec as P

F32 = jnp.float32
BF16 = jnp.bfloat16
GROUP = ("blk", "z", "core")


def from_ahead(block, axis, distance):
    size = lax.axis_size(axis)
    return lax.ppermute(block, axis, [((i + distance) % size, i) for i in range(size)])


def blk_move(block, slot, sign):
    blk, cores = lax.axis_size("blk"), lax.axis_size("core")
    route = []
    for b in range(blk):
        for c in range(cores):
            to = (b + sign * (slot + 2 * c)) % blk
            route.append((b * cores + c, to * cores + c))
    return lax.ppermute(block, ("blk", "core"), route)


def swap_core(block):
    return lax.ppermute(block, "core", [(0, 1), (1, 0)])


def shift_pieces(piece, sign):
    blk, z_size, cores = (lax.axis_size(name) for name in GROUP)
    half = z_size // 2
    route = []
    for b in range(blk):
        for z in range(z_size):
            for c in range(cores):
                to = (b + sign * (2 * c + z // half)) % blk
                route.append(((b * z_size + z) * cores + c, (to * z_size + z) * cores + c))
    return lax.ppermute(piece, GROUP, route)


def z_copies(piece):
    return jnp.broadcast_to(piece[None], (lax.axis_size("z"),) + piece.shape)


def exchange_z(copies):
    return lax.all_to_all(copies, "z", 0, 0, tiled=True)


def after(values, event):
    return lax.optimization_barrier((values, event))[0]


def pick_kernel(own_ref, picks_ref, out_ref, word_ref, bit_ref):
    own = own_ref[0]
    picks = picks_ref[...]
    place = (((own - (picks >> 9)) & 3) << 9) | (picks & 511)
    turned = jnp.transpose(place)
    word_ref[...] = turned >> 5
    bit_ref[...] = jnp.left_shift(jnp.int32(1), turned & 31)
    rows = picks_ref.shape[0]
    level = lax.broadcasted_iota(jnp.int32, (32, rows), 0)

    @pl.loop(0, out_ref.shape[1] // 128)
    def _(block):
        bits = []
        for sub in range(4):
            hit = word_ref[...] == block * 4 + sub
            total = jnp.sum(jnp.where(hit, bit_ref[...], 0), axis=0, keepdims=True)
            bits.append((jnp.broadcast_to(total, (32, rows)) >> level) & 1)
        square = jnp.concatenate(bits, 0).astype(F32)
        start = pl.multiple_of(block * 128, 128)
        out_ref[:, pl.ds(start, 128)] = jnp.transpose(square).astype(BF16)


def picked_latents(picks, own, lat_all):
    rows, count = picks.shape
    return pl.pallas_call(
        pick_kernel,
        out_shape=jax.ShapeDtypeStruct((rows, lat_all), BF16),
        in_specs=[
            pl.BlockSpec(memory_space=pltpu.SMEM),
            pl.BlockSpec(memory_space=pltpu.VMEM),
        ],
        out_specs=pl.BlockSpec(memory_space=pltpu.VMEM),
        scratch_shapes=[
            pltpu.VMEM((count, rows), jnp.int32),
            pltpu.VMEM((count, rows), jnp.int32),
        ],
        cost_estimate=pl.CostEstimate(flops=20_000_000, bytes_accessed=1_000_000, transcendentals=0),
    )(own.reshape(1).astype(jnp.int32), picks)


def two_halves(value):
    high = lax.reduce_precision(value, 8, 7)
    return [high.astype(BF16), (value - high).astype(BF16)]


def with_rows(body, rows):
    width = body.shape[1]
    rows = [jnp.pad(row, ((0, 0), (0, width - row.shape[1]))) for row in rows]
    filler = jnp.zeros((8 - len(rows), width), BF16)
    return jnp.concatenate([body] + rows + [filler], 0)


def last_rows(last, scale):
    def kernel(last_ref, loss_ref, bias_ref):
        bias_ref[...] = last_ref[0:1]
        loss_ref[0, 0] = jnp.sum(last_ref[1:3]) * scale

    vmem = pl.BlockSpec(memory_space=pltpu.VMEM)
    return pl.pallas_call(
        kernel,
        out_shape=[
            jax.ShapeDtypeStruct((1, 1), F32),
            jax.ShapeDtypeStruct((1, last.shape[1]), F32),
        ],
        in_specs=[vmem],
        out_specs=[pl.BlockSpec(memory_space=pltpu.SMEM), vmem],
    )(last)


def local(inputs, targets, enc_weight, enc_bias, dec_weight, dead_mask, aux_picks):
    blk, z_size, rep = lax.axis_size("blk"), lax.axis_size("z"), lax.axis_size("rep")
    core, blk_at, rep_at = lax.axis_index("core"), lax.axis_index("blk"), lax.axis_index("rep")
    rows, width = inputs.shape
    lat = dec_weight.shape[0]
    lat_all = blk * lat
    piece = rows * blk // (2 * z_size)
    total_tokens = rows * blk * rep
    norm_scale = 1.0 / math.sqrt(total_tokens)

    def in_slots(own, slot_1, across, slot_3):
        size = own.shape[0]
        whole = jnp.zeros((4 * size,) + own.shape[1:], own.dtype)
        for block, slot in ((own, 2 * core), (slot_1, 1), (slot_3, 3), (across, 2 - 2 * core)):
            whole = lax.dynamic_update_slice_in_dim(whole, block, slot * size, 0)
        return whole

    x_1, x_3 = blk_move(inputs, 1, -1), blk_move(inputs, 3, -1)
    x_2 = from_ahead(inputs, "blk", 2)
    enc_far = swap_core(enc_weight)
    dead = jnp.broadcast_to(dead_mask.astype(BF16)[:, None], (lat, 16))
    dec_own = jnp.concatenate([dec_weight, dead], 1)
    dec_sent, x_2 = lax.optimization_barrier((dec_own, x_2))
    x_all = in_slots(inputs, x_1, x_2, x_3)
    dec_1, dec_3 = blk_move(dec_sent, 1, 1), blk_move(dec_sent, 3, 1)
    half = dec_own.shape[1] // 32 * 16
    picked = picked_latents(aux_picks, blk_at + 2 * core, lat_all)

    x_far = swap_core(x_all[2 * rows :])
    summed = jnp.dot(x_all[: 2 * rows], enc_weight, preferred_element_type=F32)
    summed = summed + jnp.dot(x_far, enc_far, preferred_element_type=F32)
    parts = exchange_z(summed.reshape(z_size, piece, lat))
    preact = jnp.sum(parts, axis=0) + enc_bias[None, :]
    lat_piece = jnp.maximum(preact, 0.0).astype(BF16)
    lat_piece, picked = lax.optimization_barrier((lat_piece, picked))
    dec_1, dec_3 = after((dec_1, dec_3), lat_piece)
    lat_piece = shift_pieces(lat_piece, 1)
    lat_piece, passed_1, passed_3 = lax.optimization_barrier(
        (lat_piece, dec_1[:, :half], dec_3[:, half:])
    )
    dec_2 = [blk_move(passed_1, 1, 1), blk_move(passed_3, 3, 1)]
    dec_all = in_slots(dec_own, dec_1, jnp.concatenate(dec_2, 1), dec_3)
    gate = picked * dec_all[:, width][None, :]

    lat_mine = exchange_z(z_copies(lat_piece)).reshape(2, rows, lat)
    lat_other = swap_core(lat_mine)
    latents = jnp.concatenate([lat_mine[0], lat_mine[1], lat_other[0], lat_other[1]], 1)
    both = jnp.concatenate([latents, latents * gate], 0)

    decoded = jnp.dot(both, dec_all, preferred_element_type=F32)
    error = targets.astype(F32) - decoded[:rows, :width]
    error_aux = error - decoded[rows:, :width]
    squares = error * error + error_aux * error_aux
    squares = jnp.pad(squares, ((0, 0), (0, -width % 128)))
    squares = sum(squares[:, i : i + 128] for i in range(0, squares.shape[1], 128))
    loss_part = jnp.sum(squares, axis=0, keepdims=True)
    grads = jnp.concatenate(
        [(-error * norm_scale).astype(BF16), (-error_aux * norm_scale).astype(BF16)], 0
    )
    grads = jnp.pad(grads, ((0, 0), (0, dec_all.shape[1] - width)))

    def pulled_half(start):
        pulled = lax.dot_general(
            grads,
            dec_all[start : start + 2 * lat],
            (((1,), (1,)), ((), ())),
            preferred_element_type=F32,
        )
        return pulled[:rows] + pulled[rows:] * gate[:, start : start + 2 * lat].astype(F32)

    got_pulled = swap_core(pulled_half(2 * lat).astype(BF16)).astype(F32)
    pulled_sum = pulled_half(0) + got_pulled
    quarters = rows // piece
    pulled_sum = pulled_sum.astype(BF16).reshape(quarters, piece, 2, lat // 128, 128)
    pulled_sum = jnp.transpose(pulled_sum, (2, 0, 3, 1, 4)).reshape(z_size, piece * lat // 128, 128)
    loss_rows = jnp.concatenate(two_halves(loss_part) + [jnp.zeros((6, 128), BF16)], 0)
    loss_rows = jnp.broadcast_to(loss_rows[None], (z_size,) + loss_rows.shape)
    packet = jnp.concatenate([pulled_sum, loss_rows], 1)
    arrived = exchange_z(packet).astype(F32)

    dec_term = lax.dot_general(
        after(grads, packet), both, (((0,), (0,)), ((), ())), preferred_element_type=F32
    ).astype(BF16)
    share = width // rep

    def rep_exchange(shares):
        own = lax.dynamic_index_in_dim(shares, rep_at, 0, False)
        parts = [own]
        for step in (1, 3, 2):
            outgoing = lax.dynamic_index_in_dim(shares, (rep_at + step) % rep, 0, False)
            parts.append(from_ahead(outgoing, "rep", -step))
        return parts

    dec_parts = rep_exchange(dec_term[:width].reshape(rep, share, lat_all))

    arrived = jnp.sum(arrived, axis=0)
    grad_piece = arrived[:-8].reshape(lat // 128, piece, 128)
    grad_piece = jnp.concatenate([grad_piece[i] for i in range(lat // 128)], 1)
    grad_piece = jnp.where(lat_piece > 0, grad_piece, 0.0).astype(BF16)
    loss_width = arrived[-8:-7] + arrived[-7:-6]
    grad_piece = shift_pieces(grad_piece, -1)
    grad_copies = z_copies(grad_piece)
    loss_width = after(loss_width, grad_copies)
    loss_width = loss_width + swap_core(loss_width)
    dec_sum = sum(part.astype(F32) for part in after(dec_parts, grad_copies)).astype(BF16)

    loss_out = two_halves(loss_width)
    dec_own_slot = lax.dynamic_slice_in_dim(dec_sum, core * 2 * lat, lat, 1)
    dec_across = lax.dynamic_slice_in_dim(dec_sum, (1 - core) * 2 * lat, lat, 1)
    incoming = [
        blk_move(with_rows(dec_sum[:, lat : 2 * lat], loss_out), 1, -1),
        blk_move(with_rows(dec_sum[:, 3 * lat :], loss_out), 3, -1),
        from_ahead(with_rows(dec_across, loss_out), "blk", 2),
    ]

    grad_mine = exchange_z(grad_copies).reshape(2 * rows, lat)
    incoming = after(incoming, grad_mine)
    dec_final = dec_own_slot.astype(F32) + sum(part[:share].astype(F32) for part in incoming)
    loss_blk = loss_width
    for part in incoming:
        both_rows = part[share : share + 2, :128].astype(F32)
        loss_blk = loss_blk + both_rows[0:1] + both_rows[1:2]
    grad_dec = jnp.transpose(dec_final)
    grad_pre = jnp.concatenate([grad_mine, swap_core(grad_mine)], 0)
    enc_term = lax.dot_general(
        x_all, grad_pre, (((0,), (0,)), ((), ())), preferred_element_type=F32
    ).astype(BF16)
    bias_term = jnp.sum(grad_pre.astype(F32), axis=0, keepdims=True).astype(BF16)

    quarter = lat // rep
    more = [bias_term.reshape(rep, 1, quarter)]
    more += [jnp.broadcast_to(row[None], (rep,) + row.shape) for row in two_halves(loss_blk)]
    more = [jnp.pad(row, ((0, 0), (0, 0), (0, lat - row.shape[2]))) for row in more]
    more.append(jnp.zeros((rep, 5, lat), BF16))
    parts = rep_exchange(jnp.concatenate([enc_term.reshape(rep, share, lat)] + more, 1))
    grad_enc = sum(part[:share].astype(F32) for part in parts)
    last = sum(part[share : share + 3, :quarter].astype(F32) for part in parts)
    loss, bias = last_rows(last, 1.0 / (total_tokens * width * 2 * z_size))
    return (loss.reshape(()), grad_enc, bias.reshape(quarter), grad_dec)


def solution(mesh):
    sizes = mesh.shape
    fine = Mesh(
        mesh.devices.reshape(sizes["blk"], sizes["width"] // 2, 2, sizes["rep"]),
        ("blk", "z", "core", "rep"),
    )
    wide = ("z", "core")
    in_specs = (
        P(("blk", "rep"), wide),
        P(("blk", "rep"), wide),
        P(wide, "blk"),
        P("blk"),
        P("blk", wide),
        P("blk"),
        P(("blk", "rep"), None),
    )
    out_specs = (P(), P(wide + ("rep",), "blk"), P(("blk", "rep")), P("blk", wide + ("rep",)))
    return jax.shard_map(local, mesh=fine, in_specs=in_specs, out_specs=out_specs, check_vma=False)
```

```python
import math

import jax
import jax.numpy as jnp
from jax import lax
from jax.experimental import pallas as pl
from jax.experimental.pallas import tpu as pltpu
from jax.sharding import Mesh, PartitionSpec as P

F32 = jnp.float32
BF16 = jnp.bfloat16
GROUP = ("blk", "z", "core")


def from_ahead(block, axis, distance):
    size = lax.axis_size(axis)
    return lax.ppermute(block, axis, [((i + distance) % size, i) for i in range(size)])


def blk_move(block, slot, sign):
    blk, cores = lax.axis_size("blk"), lax.axis_size("core")
    route = []
    for b in range(blk):
        for c in range(cores):
            to = (b + sign * (slot + 2 * c)) % blk
            route.append((b * cores + c, to * cores + c))
    return lax.ppermute(block, ("blk", "core"), route)


def swap_core(block):
    return lax.ppermute(block, "core", [(0, 1), (1, 0)])


def shift_pieces(piece, sign):
    blk, z_size, cores = (lax.axis_size(name) for name in GROUP)
    half = z_size // 2
    route = []
    for b in range(blk):
        for z in range(z_size):
            for c in range(cores):
                to = (b + sign * (2 * c + z // half)) % blk
                route.append(((b * z_size + z) * cores + c, (to * z_size + z) * cores + c))
    return lax.ppermute(piece, GROUP, route)


def z_copies(piece):
    return jnp.broadcast_to(piece[None], (lax.axis_size("z"),) + piece.shape)


def exchange_z(copies):
    return lax.all_to_all(copies, "z", 0, 0, tiled=True)


def after(values, event):
    return lax.optimization_barrier((values, event))[0]


def pick_kernel(own_ref, picks_ref, out_ref, word_ref, bit_ref):
    own = own_ref[0]
    picks = picks_ref[...]
    place = (((own - (picks >> 9)) & 3) << 9) | (picks & 511)
    turned = jnp.transpose(place)
    word_ref[...] = turned >> 5
    bit_ref[...] = jnp.left_shift(jnp.int32(1), turned & 31)
    rows = picks_ref.shape[0]
    level = lax.broadcasted_iota(jnp.int32, (32, rows), 0)

    @pl.loop(0, out_ref.shape[1] // 128)
    def _(block):
        bits = []
        for sub in range(4):
            hit = word_ref[...] == block * 4 + sub
            total = jnp.sum(jnp.where(hit, bit_ref[...], 0), axis=0, keepdims=True)
            bits.append((jnp.broadcast_to(total, (32, rows)) >> level) & 1)
        square = jnp.concatenate(bits, 0).astype(F32)
        start = pl.multiple_of(block * 128, 128)
        out_ref[:, pl.ds(start, 128)] = jnp.transpose(square).astype(BF16)


def picked_latents(picks, own, lat_all):
    rows, count = picks.shape
    return pl.pallas_call(
        pick_kernel,
        out_shape=jax.ShapeDtypeStruct((rows, lat_all), BF16),
        in_specs=[
            pl.BlockSpec(memory_space=pltpu.SMEM),
            pl.BlockSpec(memory_space=pltpu.VMEM),
        ],
        out_specs=pl.BlockSpec(memory_space=pltpu.VMEM),
        scratch_shapes=[
            pltpu.VMEM((count, rows), jnp.int32),
            pltpu.VMEM((count, rows), jnp.int32),
        ],
        cost_estimate=pl.CostEstimate(flops=20_000_000, bytes_accessed=1_000_000, transcendentals=0),
    )(own.reshape(1).astype(jnp.int32), picks)


def two_halves(value):
    high = lax.reduce_precision(value, 8, 7)
    return [high.astype(BF16), (value - high).astype(BF16)]


def with_rows(body, rows):
    width = body.shape[1]
    rows = [jnp.pad(row, ((0, 0), (0, width - row.shape[1]))) for row in rows]
    filler = jnp.zeros((8 - len(rows), width), BF16)
    return jnp.concatenate([body] + rows + [filler], 0)


def last_rows(last, scale):
    def kernel(last_ref, loss_ref, bias_ref):
        bias_ref[...] = last_ref[0:1]
        loss_ref[0, 0] = jnp.sum(last_ref[1:3]) * scale

    vmem = pl.BlockSpec(memory_space=pltpu.VMEM)
    return pl.pallas_call(
        kernel,
        out_shape=[
            jax.ShapeDtypeStruct((1, 1), F32),
            jax.ShapeDtypeStruct((1, last.shape[1]), F32),
        ],
        in_specs=[vmem],
        out_specs=[pl.BlockSpec(memory_space=pltpu.SMEM), vmem],
    )(last)


def local(inputs, targets, enc_weight, enc_bias, dec_weight, dead_mask, aux_picks):
    blk, z_size, rep = lax.axis_size("blk"), lax.axis_size("z"), lax.axis_size("rep")
    core, blk_at, rep_at = lax.axis_index("core"), lax.axis_index("blk"), lax.axis_index("rep")
    rows, width = inputs.shape
    lat = dec_weight.shape[0]
    lat_all = blk * lat
    piece = rows * blk // (2 * z_size)
    total_tokens = rows * blk * rep
    norm_scale = 1.0 / math.sqrt(total_tokens)

    def in_slots(own, slot_1, across, slot_3):
        size = own.shape[0]
        whole = jnp.zeros((4 * size,) + own.shape[1:], own.dtype)
        for block, slot in ((own, 2 * core), (slot_1, 1), (slot_3, 3), (across, 2 - 2 * core)):
            whole = lax.dynamic_update_slice_in_dim(whole, block, slot * size, 0)
        return whole

    x_1, x_3 = blk_move(inputs, 1, -1), blk_move(inputs, 3, -1)
    x_2 = from_ahead(inputs, "blk", 2)
    enc_far = swap_core(enc_weight)
    dead = jnp.broadcast_to(dead_mask.astype(BF16)[:, None], (lat, 16))
    dec_own = jnp.concatenate([dec_weight, dead], 1)
    dec_sent, x_2 = lax.optimization_barrier((dec_own, x_2))
    x_all = in_slots(inputs, x_1, x_2, x_3)
    dec_1, dec_3 = blk_move(dec_sent, 1, 1), blk_move(dec_sent, 3, 1)
    half = dec_own.shape[1] // 32 * 16
    picked = picked_latents(aux_picks, blk_at + 2 * core, lat_all)

    x_far = swap_core(x_all[2 * rows :])
    summed = jnp.dot(x_all[: 2 * rows], enc_weight, preferred_element_type=F32)
    summed = summed + jnp.dot(x_far, enc_far, preferred_element_type=F32)
    parts = exchange_z(summed.reshape(z_size, piece, lat))
    preact = jnp.sum(parts, axis=0) + enc_bias[None, :]
    lat_piece = jnp.maximum(preact, 0.0).astype(BF16)
    lat_piece, picked = lax.optimization_barrier((lat_piece, picked))
    lat_piece = shift_pieces(lat_piece, 1)
    lat_copies = z_copies(lat_piece)
    dec_1, dec_3 = after((dec_1, dec_3), lat_copies)
    dec_2 = [blk_move(dec_1[:, :half], 1, 1), blk_move(dec_3[:, half:], 3, 1)]
    dec_all = in_slots(dec_own, dec_1, jnp.concatenate(dec_2, 1), dec_3)
    gate = picked * dec_all[:, width][None, :]

    lat_mine = exchange_z(lat_copies).reshape(2, rows, lat)
    lat_other = swap_core(lat_mine)
    latents = jnp.concatenate([lat_mine[0], lat_mine[1], lat_other[0], lat_other[1]], 1)
    both = jnp.concatenate([latents, latents * gate], 0)

    decoded = jnp.dot(both, dec_all, preferred_element_type=F32)
    error = targets.astype(F32) - decoded[:rows, :width]
    error_aux = error - decoded[rows:, :width]
    squares = error * error + error_aux * error_aux
    squares = jnp.pad(squares, ((0, 0), (0, -width % 128)))
    squares = sum(squares[:, i : i + 128] for i in range(0, squares.shape[1], 128))
    loss_part = jnp.sum(squares, axis=0, keepdims=True)
    grads = jnp.concatenate(
        [(-error * norm_scale).astype(BF16), (-error_aux * norm_scale).astype(BF16)], 0
    )
    grads = jnp.pad(grads, ((0, 0), (0, dec_all.shape[1] - width)))

    def pulled_half(start):
        pulled = lax.dot_general(
            grads,
            dec_all[start : start + 2 * lat],
            (((1,), (1,)), ((), ())),
            preferred_element_type=F32,
        )
        return pulled[:rows] + pulled[rows:] * gate[:, start : start + 2 * lat].astype(F32)

    got_pulled = swap_core(pulled_half(2 * lat).astype(BF16)).astype(F32)
    pulled_sum = pulled_half(0) + got_pulled
    quarters = rows // piece
    pulled_sum = pulled_sum.astype(BF16).reshape(quarters, piece, 2, lat // 128, 128)
    pulled_sum = jnp.transpose(pulled_sum, (2, 0, 3, 1, 4)).reshape(z_size, piece * lat // 128, 128)
    loss_rows = jnp.concatenate(two_halves(loss_part) + [jnp.zeros((6, 128), BF16)], 0)
    loss_rows = jnp.broadcast_to(loss_rows[None], (z_size,) + loss_rows.shape)
    packet = jnp.concatenate([pulled_sum, loss_rows], 1)
    arrived = exchange_z(packet).astype(F32)

    dec_term = lax.dot_general(
        after(grads, packet), both, (((0,), (0,)), ((), ())), preferred_element_type=F32
    ).astype(BF16)
    share = width // rep

    def rep_exchange(shares):
        own = lax.dynamic_index_in_dim(shares, rep_at, 0, False)
        parts = [own]
        for step in (1, 3, 2):
            outgoing = lax.dynamic_index_in_dim(shares, (rep_at + step) % rep, 0, False)
            parts.append(from_ahead(outgoing, "rep", -step))
        return parts

    dec_parts = rep_exchange(dec_term[:width].reshape(rep, share, lat_all))

    arrived = jnp.sum(arrived, axis=0)
    grad_piece = arrived[:-8].reshape(lat // 128, piece, 128)
    grad_piece = jnp.concatenate([grad_piece[i] for i in range(lat // 128)], 1)
    grad_piece = jnp.where(lat_piece > 0, grad_piece, 0.0).astype(BF16)
    loss_width = arrived[-8:-7] + arrived[-7:-6]
    grad_piece = shift_pieces(grad_piece, -1)
    grad_copies = z_copies(grad_piece)
    loss_width = after(loss_width, grad_copies)
    loss_width = loss_width + swap_core(loss_width)
    dec_sum = sum(part.astype(F32) for part in after(dec_parts, grad_copies)).astype(BF16)

    loss_out = two_halves(loss_width)
    dec_own_slot = lax.dynamic_slice_in_dim(dec_sum, core * 2 * lat, lat, 1)
    dec_across = lax.dynamic_slice_in_dim(dec_sum, (1 - core) * 2 * lat, lat, 1)
    incoming = [
        blk_move(with_rows(dec_sum[:, lat : 2 * lat], loss_out), 1, -1),
        blk_move(with_rows(dec_sum[:, 3 * lat :], loss_out), 3, -1),
        from_ahead(with_rows(dec_across, loss_out), "blk", 2),
    ]

    grad_mine = exchange_z(grad_copies).reshape(2 * rows, lat)
    incoming = after(incoming, grad_mine)
    dec_final = dec_own_slot.astype(F32) + sum(part[:share].astype(F32) for part in incoming)
    loss_blk = loss_width
    for part in incoming:
        both_rows = part[share : share + 2, :128].astype(F32)
        loss_blk = loss_blk + both_rows[0:1] + both_rows[1:2]
    grad_dec = jnp.transpose(dec_final)
    grad_pre = jnp.concatenate([grad_mine, swap_core(grad_mine)], 0)
    enc_term = lax.dot_general(
        x_all, grad_pre, (((0,), (0,)), ((), ())), preferred_element_type=F32
    ).astype(BF16)
    bias_term = jnp.sum(grad_pre.astype(F32), axis=0, keepdims=True).astype(BF16)

    quarter = lat // rep
    more = [bias_term.reshape(rep, 1, quarter)]
    more += [jnp.broadcast_to(row[None], (rep,) + row.shape) for row in two_halves(loss_blk)]
    more = [jnp.pad(row, ((0, 0), (0, 0), (0, lat - row.shape[2]))) for row in more]
    more.append(jnp.zeros((rep, 5, lat), BF16))
    parts = rep_exchange(jnp.concatenate([enc_term.reshape(rep, share, lat)] + more, 1))
    grad_enc = sum(part[:share].astype(F32) for part in parts)
    last = sum(part[share : share + 3, :quarter].astype(F32) for part in parts)
    loss, bias = last_rows(last, 1.0 / (total_tokens * width * 2 * z_size))
    return (loss.reshape(()), grad_enc, bias.reshape(quarter), grad_dec)


def solution(mesh):
    sizes = mesh.shape
    fine = Mesh(
        mesh.devices.reshape(sizes["blk"], sizes["width"] // 2, 2, sizes["rep"]),
        ("blk", "z", "core", "rep"),
    )
    wide = ("z", "core")
    in_specs = (
        P(("blk", "rep"), wide),
        P(("blk", "rep"), wide),
        P(wide, "blk"),
        P("blk"),
        P("blk", wide),
        P("blk"),
        P(("blk", "rep"), None),
    )
    out_specs = (P(), P(wide + ("rep",), "blk"), P(("blk", "rep")), P("blk", wide + ("rep",)))
    return jax.shard_map(local, mesh=fine, in_specs=in_specs, out_specs=out_specs, check_vma=False)
```

```python
import math

import jax
import jax.numpy as jnp
from jax import lax
from jax.experimental import pallas as pl
from jax.experimental.pallas import tpu as pltpu
from jax.sharding import Mesh, PartitionSpec as P

F32 = jnp.float32
BF16 = jnp.bfloat16
GROUP = ("blk", "z", "core")


def from_ahead(block, axis, distance):
    size = lax.axis_size(axis)
    return lax.ppermute(block, axis, [((i + distance) % size, i) for i in range(size)])


def blk_move(block, slot, sign):
    blk, cores = lax.axis_size("blk"), lax.axis_size("core")
    route = []
    for b in range(blk):
        for c in range(cores):
            to = (b + sign * (slot + 2 * c)) % blk
            route.append((b * cores + c, to * cores + c))
    return lax.ppermute(block, ("blk", "core"), route)


def swap_core(block):
    return lax.ppermute(block, "core", [(0, 1), (1, 0)])


def shift_pieces(piece, sign):
    blk, z_size, cores = (lax.axis_size(name) for name in GROUP)
    half = z_size // 2
    route = []
    for b in range(blk):
        for z in range(z_size):
            for c in range(cores):
                to = (b + sign * (2 * c + z // half)) % blk
                route.append(((b * z_size + z) * cores + c, (to * z_size + z) * cores + c))
    return lax.ppermute(piece, GROUP, route)


def z_copies(piece):
    return jnp.broadcast_to(piece[None], (lax.axis_size("z"),) + piece.shape)


def exchange_z(copies):
    return lax.all_to_all(copies, "z", 0, 0, tiled=True)


def after(values, event):
    return lax.optimization_barrier((values, event))[0]


def pick_kernel(own_ref, picks_ref, out_ref, word_ref, bit_ref):
    own = own_ref[0]
    picks = picks_ref[...]
    place = (((own - (picks >> 9)) & 3) << 9) | (picks & 511)
    turned = jnp.transpose(place)
    word_ref[...] = turned >> 5
    bit_ref[...] = jnp.left_shift(jnp.int32(1), turned & 31)
    rows = picks_ref.shape[0]
    level = lax.broadcasted_iota(jnp.int32, (32, rows), 0)

    @pl.loop(0, out_ref.shape[1] // 128)
    def _(block):
        bits = []
        for sub in range(4):
            hit = word_ref[...] == block * 4 + sub
            total = jnp.sum(jnp.where(hit, bit_ref[...], 0), axis=0, keepdims=True)
            bits.append((jnp.broadcast_to(total, (32, rows)) >> level) & 1)
        square = jnp.concatenate(bits, 0).astype(F32)
        start = pl.multiple_of(block * 128, 128)
        out_ref[:, pl.ds(start, 128)] = jnp.transpose(square).astype(BF16)


def picked_latents(picks, own, lat_all):
    rows, count = picks.shape
    return pl.pallas_call(
        pick_kernel,
        out_shape=jax.ShapeDtypeStruct((rows, lat_all), BF16),
        in_specs=[
            pl.BlockSpec(memory_space=pltpu.SMEM),
            pl.BlockSpec(memory_space=pltpu.VMEM),
        ],
        out_specs=pl.BlockSpec(memory_space=pltpu.VMEM),
        scratch_shapes=[
            pltpu.VMEM((count, rows), jnp.int32),
            pltpu.VMEM((count, rows), jnp.int32),
        ],
        cost_estimate=pl.CostEstimate(flops=20_000_000, bytes_accessed=1_000_000, transcendentals=0),
    )(own.reshape(1).astype(jnp.int32), picks)


def two_halves(value):
    high = lax.reduce_precision(value, 8, 7)
    return [high.astype(BF16), (value - high).astype(BF16)]


def with_rows(body, rows):
    width = body.shape[1]
    rows = [jnp.pad(row, ((0, 0), (0, width - row.shape[1]))) for row in rows]
    filler = jnp.zeros((8 - len(rows), width), BF16)
    return jnp.concatenate([body] + rows + [filler], 0)


def last_rows(last, scale):
    def kernel(last_ref, loss_ref, bias_ref):
        bias_ref[...] = last_ref[0:1]
        loss_ref[0, 0] = jnp.sum(last_ref[1:3]) * scale

    vmem = pl.BlockSpec(memory_space=pltpu.VMEM)
    return pl.pallas_call(
        kernel,
        out_shape=[
            jax.ShapeDtypeStruct((1, 1), F32),
            jax.ShapeDtypeStruct((1, last.shape[1]), F32),
        ],
        in_specs=[vmem],
        out_specs=[pl.BlockSpec(memory_space=pltpu.SMEM), vmem],
    )(last)


def local(inputs, targets, enc_weight, enc_bias, dec_weight, dead_mask, aux_picks):
    blk, z_size, rep = lax.axis_size("blk"), lax.axis_size("z"), lax.axis_size("rep")
    core, blk_at, rep_at = lax.axis_index("core"), lax.axis_index("blk"), lax.axis_index("rep")
    rows, width = inputs.shape
    lat = dec_weight.shape[0]
    lat_all = blk * lat
    piece = rows * blk // (2 * z_size)
    total_tokens = rows * blk * rep
    norm_scale = 1.0 / math.sqrt(total_tokens)

    def in_slots(own, slot_1, across, slot_3):
        size = own.shape[0]
        whole = jnp.zeros((4 * size,) + own.shape[1:], own.dtype)
        for block, slot in ((own, 2 * core), (slot_1, 1), (slot_3, 3), (across, 2 - 2 * core)):
            whole = lax.dynamic_update_slice_in_dim(whole, block, slot * size, 0)
        return whole

    x_1, x_3 = blk_move(inputs, 1, -1), blk_move(inputs, 3, -1)
    x_2 = from_ahead(inputs, "blk", 2)
    enc_far = swap_core(enc_weight)
    dead = jnp.broadcast_to(dead_mask.astype(BF16)[:, None], (lat, 16))
    dec_own = jnp.concatenate([dec_weight, dead], 1)
    dec_sent, x_2 = lax.optimization_barrier((dec_own, x_2))
    x_all = in_slots(inputs, x_1, x_2, x_3)
    dec_1, dec_3 = blk_move(dec_sent, 1, 1), blk_move(dec_sent, 3, 1)
    half = dec_own.shape[1] // 32 * 16
    picked = picked_latents(aux_picks, blk_at + 2 * core, lat_all)

    far_2, far_3 = swap_core(x_all[2 * rows : 3 * rows]), swap_core(x_3)
    x_far = jnp.concatenate([far_2, far_3], 0)
    summed = jnp.dot(x_all[: 2 * rows], enc_weight, preferred_element_type=F32)
    summed = summed + jnp.dot(x_far, enc_far, preferred_element_type=F32)
    parts = exchange_z(summed.reshape(z_size, piece, lat))
    preact = jnp.sum(parts, axis=0) + enc_bias[None, :]
    lat_piece = jnp.maximum(preact, 0.0).astype(BF16)
    lat_piece, picked = lax.optimization_barrier((lat_piece, picked))
    dec_1, dec_3 = after((dec_1, dec_3), lat_piece)
    lat_piece = shift_pieces(lat_piece, 1)
    lat_piece, passed_1, passed_3 = lax.optimization_barrier(
        (lat_piece, dec_1[:, :half], dec_3[:, half:])
    )
    dec_2 = [blk_move(passed_1, 1, 1), blk_move(passed_3, 3, 1)]
    dec_all = in_slots(dec_own, dec_1, jnp.concatenate(dec_2, 1), dec_3)
    gate = picked * dec_all[:, width][None, :]

    lat_mine = exchange_z(z_copies(lat_piece)).reshape(2, rows, lat)
    lat_other = swap_core(lat_mine)
    latents = jnp.concatenate([lat_mine[0], lat_mine[1], lat_other[0], lat_other[1]], 1)
    both = jnp.concatenate([latents, latents * gate], 0)

    decoded = jnp.dot(both, dec_all, preferred_element_type=F32)
    error = targets.astype(F32) - decoded[:rows, :width]
    error_aux = error - decoded[rows:, :width]
    squares = error * error + error_aux * error_aux
    squares = jnp.pad(squares, ((0, 0), (0, -width % 128)))
    squares = sum(squares[:, i : i + 128] for i in range(0, squares.shape[1], 128))
    loss_part = jnp.sum(squares, axis=0, keepdims=True)
    grads = jnp.concatenate(
        [(-error * norm_scale).astype(BF16), (-error_aux * norm_scale).astype(BF16)], 0
    )
    grads = jnp.pad(grads, ((0, 0), (0, dec_all.shape[1] - width)))

    def pulled_half(start):
        pulled = lax.dot_general(
            grads,
            dec_all[start : start + 2 * lat],
            (((1,), (1,)), ((), ())),
            preferred_element_type=F32,
        )
        return pulled[:rows] + pulled[rows:] * gate[:, start : start + 2 * lat].astype(F32)

    got_pulled = swap_core(pulled_half(2 * lat).astype(BF16)).astype(F32)
    pulled_sum = pulled_half(0) + got_pulled
    quarters = rows // piece
    pulled_sum = pulled_sum.astype(BF16).reshape(quarters, piece, 2, lat // 128, 128)
    pulled_sum = jnp.transpose(pulled_sum, (2, 0, 3, 1, 4)).reshape(z_size, piece * lat // 128, 128)
    loss_rows = jnp.concatenate(two_halves(loss_part) + [jnp.zeros((6, 128), BF16)], 0)
    loss_rows = jnp.broadcast_to(loss_rows[None], (z_size,) + loss_rows.shape)
    packet = jnp.concatenate([pulled_sum, loss_rows], 1)
    arrived = exchange_z(packet).astype(F32)

    dec_term = lax.dot_general(
        after(grads, packet), both, (((0,), (0,)), ((), ())), preferred_element_type=F32
    ).astype(BF16)
    share = width // rep

    def rep_exchange(shares):
        own = lax.dynamic_index_in_dim(shares, rep_at, 0, False)
        parts = [own]
        for step in (1, 3, 2):
            outgoing = lax.dynamic_index_in_dim(shares, (rep_at + step) % rep, 0, False)
            parts.append(from_ahead(outgoing, "rep", -step))
        return parts

    dec_parts = rep_exchange(dec_term[:width].reshape(rep, share, lat_all))

    arrived = jnp.sum(arrived, axis=0)
    grad_piece = arrived[:-8].reshape(lat // 128, piece, 128)
    grad_piece = jnp.concatenate([grad_piece[i] for i in range(lat // 128)], 1)
    grad_piece = jnp.where(lat_piece > 0, grad_piece, 0.0).astype(BF16)
    loss_width = arrived[-8:-7] + arrived[-7:-6]
    grad_piece = shift_pieces(grad_piece, -1)
    grad_copies = z_copies(grad_piece)
    loss_width = after(loss_width, grad_copies)
    loss_width = loss_width + swap_core(loss_width)
    dec_sum = sum(part.astype(F32) for part in after(dec_parts, grad_copies)).astype(BF16)

    loss_out = two_halves(loss_width)
    dec_own_slot = lax.dynamic_slice_in_dim(dec_sum, core * 2 * lat, lat, 1)
    dec_across = lax.dynamic_slice_in_dim(dec_sum, (1 - core) * 2 * lat, lat, 1)
    incoming = [
        blk_move(with_rows(dec_sum[:, lat : 2 * lat], loss_out), 1, -1),
        blk_move(with_rows(dec_sum[:, 3 * lat :], loss_out), 3, -1),
        from_ahead(with_rows(dec_across, loss_out), "blk", 2),
    ]

    grad_mine = exchange_z(grad_copies).reshape(2 * rows, lat)
    incoming = after(incoming, grad_mine)
    dec_final = dec_own_slot.astype(F32) + sum(part[:share].astype(F32) for part in incoming)
    loss_blk = loss_width
    for part in incoming:
        both_rows = part[share : share + 2, :128].astype(F32)
        loss_blk = loss_blk + both_rows[0:1] + both_rows[1:2]
    grad_dec = jnp.transpose(dec_final)
    grad_pre = jnp.concatenate([grad_mine, swap_core(grad_mine)], 0)
    enc_term = lax.dot_general(
        x_all, grad_pre, (((0,), (0,)), ((), ())), preferred_element_type=F32
    ).astype(BF16)
    bias_term = jnp.sum(grad_pre.astype(F32), axis=0, keepdims=True).astype(BF16)

    quarter = lat // rep
    more = [bias_term.reshape(rep, 1, quarter)]
    more += [jnp.broadcast_to(row[None], (rep,) + row.shape) for row in two_halves(loss_blk)]
    more = [jnp.pad(row, ((0, 0), (0, 0), (0, lat - row.shape[2]))) for row in more]
    more.append(jnp.zeros((rep, 5, lat), BF16))
    parts = rep_exchange(jnp.concatenate([enc_term.reshape(rep, share, lat)] + more, 1))
    grad_enc = sum(part[:share].astype(F32) for part in parts)
    last = sum(part[share : share + 3, :quarter].astype(F32) for part in parts)
    loss, bias = last_rows(last, 1.0 / (total_tokens * width * 2 * z_size))
    return (loss.reshape(()), grad_enc, bias.reshape(quarter), grad_dec)


def solution(mesh):
    sizes = mesh.shape
    fine = Mesh(
        mesh.devices.reshape(sizes["blk"], sizes["width"] // 2, 2, sizes["rep"]),
        ("blk", "z", "core", "rep"),
    )
    wide = ("z", "core")
    in_specs = (
        P(("blk", "rep"), wide),
        P(("blk", "rep"), wide),
        P(wide, "blk"),
        P("blk"),
        P("blk", wide),
        P("blk"),
        P(("blk", "rep"), None),
    )
    out_specs = (P(), P(wide + ("rep",), "blk"), P(("blk", "rep")), P("blk", wide + ("rep",)))
    return jax.shard_map(local, mesh=fine, in_specs=in_specs, out_specs=out_specs, check_vma=False)
```
